32 devices in a mesh: slab: 16 (over z, x, core), blk: 2 (over y).
Axes of the slice: x: 2, y: 2, z: 4, core: 2. Of those that a mesh axis runs over, the one named last changes fastest.
Arguments:
- modes: bfloat16 [65536, 2048], P('slab', 'blk'), may hold values from -6 to 6
- stiffness: bfloat16 [65536, 512], P('slab'), may hold values from -0.0009765625 to 0.0009765625
- offsets: int32 [1024, 8], P('slab'), may hold values from -4 to 4, as said below
Outputs:
- reduced: float32 [2048, 2048], P('blk', 'slab')
The draws below stay inside these ranges and needn't reach their ends.
Inputs may be any that keep to these rules, and one draw needn't show every extreme that they name: Each row of offsets lists 8 different values, in an order drawn from the seed: all of -4 to 4 except one nonzero value of magnitude below 4.
All inputs are finite; a program needn't handle non-finite values.
Results may differ from the reference program's by a relative error of at most 0.0029.
Values may be sent and summed in bfloat16 or wider, within the bound.
No kernel may reach another device: no remote copies, remote signals or barrier semaphores. Data moves between devices by JAX's collectives and lax.ppermute only.
A program may use at most 192 MiB of HBM per device.

```python
import jax
import jax.numpy as jnp
from jax import lax

M = 2048
BS = 64
HB = 4
BPR = 8
NDOF = 65536
NBR = 1024


def draw_offsets(key, part):
    row_keys = jax.random.split(key, NBR)
    magnitude = jax.random.randint(jax.random.fold_in(key, 7), (NBR,), 1, HB)
    signs = jax.random.randint(jax.random.fold_in(key, 11), (NBR,), 0, 2) * 2 - 1
    dropped = magnitude * signs
    slots = jnp.arange(BPR, dtype=jnp.int32)
    values = -HB + slots[None, :] + (slots[None, :] >= (dropped + HB)[:, None]).astype(jnp.int32)
    orders = jax.vmap(lambda k: jax.random.permutation(k, BPR))(row_keys)
    return jnp.take_along_axis(values, orders, axis=1).astype(jnp.int32)


def with_spikes(array, stream_key, source, target, blocks, factor):
    def block_of(axis_at):
        return (jnp.arange(array.shape[axis_at]) // (array.shape[axis_at] // blocks)).reshape((-1,) + (1,) * (array.ndim - 1 - axis_at))

    one_side = jax.random.permutation(stream_key, blocks)[block_of(target)]
    far = (block_of(target) + blocks // 2) % blocks
    return jnp.where((block_of(source) == one_side) | (block_of(source) == far), factor * array, array)


def block_levels(own_key, extent, shards, least, top_value):
    gain = 1.0
    for dim, blocks in shards:
        steps = jax.random.uniform(jax.random.fold_in(jax.random.fold_in(own_key, 6), dim), (blocks,), jnp.float32, least / len(shards), top_value / len(shards))
        gain = gain * jnp.repeat(jnp.exp(steps), extent[dim] // blocks).reshape((-1,) + (1,) * (len(extent) - 1 - dim))
    return gain


def centred(rng, shape, deviation, reach, cuts=(), kind=jnp.bfloat16):
    entries = jax.random.normal(rng, shape, jnp.float32) * deviation
    if len(cuts) > 0:
        entries = block_levels(rng, shape, cuts, -0.22, 0.18) * entries
    return jnp.clip(entries, min=-reach, max=reach).astype(kind)


def heavy_noise(stream_key, dims, scale, reach, shards, heavy, kind=jnp.bfloat16):
    result = scale * jax.random.normal(stream_key, dims, jnp.float32)
    if shards:
        result = result * block_levels(stream_key, dims, shards, -0.22, 0.18)
    return jnp.clip(with_spikes(result, jax.random.fold_in(stream_key, 3), *heavy), -reach, reach).astype(kind)


def setup_inputs(seed: int = 0) -> dict:
    splits = jax.random.split(jax.random.key(seed), 4)
    return {
        "modes": heavy_noise(splits[0], (NDOF, M), 1.0, 6.0, ((0, 16), (1, 2)), (0, 1, 16, 2.0)),
        "stiffness": centred(splits[1], (NDOF, BPR * BS), (BPR * BS * NDOF) ** -0.5, 0.0009765625, ((0, 16),)),
        "offsets": draw_offsets(jax.random.fold_in(splits[3], 71), 0),
    }


def reference(modes, stiffness, offsets):
    rim = HB * BS
    padded = jnp.pad(modes.astype(jnp.float32), ((rim, rim), (0, 0)))
    blocks = padded.reshape(NBR + 2 * HB, BS, M)
    kblocks = stiffness.astype(jnp.float32).reshape(NBR, BS, BPR, BS)
    base = jnp.arange(NBR, dtype=jnp.int32)
    total = jnp.zeros((NBR, BS, M), jnp.float32)
    for column in range(BPR):
        where = (base + offsets[:, column] + HB).astype(jnp.int32)
        picked = jnp.take(blocks, where, axis=0)
        total = total + jnp.einsum("nab,nbm->nam", kblocks[:, :, column, :], picked, precision=lax.Precision.HIGHEST)
    kphi = total.reshape(NDOF, M).astype(jnp.bfloat16)
    return jnp.dot(modes.T, kphi, preferred_element_type=jnp.float32)
```

```python
import functools

import jax
import jax.numpy as jnp
from jax import lax
from jax.experimental import pallas as pl
from jax.experimental.pallas import tpu as pltpu
from jax.sharding import PartitionSpec as P

BS = 64
HB = 4
BPR = 8
TILE = HB * BS
BAND = 3 * TILE
AXES = ("slab", "blk")
F32 = jnp.float32
BF16 = jnp.bfloat16
NT = (((1,), (1,)), ((), ()))
TN = (((0,), (0,)), ((), ()))
VMEM_LIMIT = 56 * 1024 * 1024


def dot(a, b, dims=(((1,), (0,)), ((), ()))):
    return lax.dot_general(a, b, dims, preferred_element_type=F32)


def params():
    return pltpu.CompilerParams(vmem_limit_bytes=VMEM_LIMIT, dimension_semantics=("arbitrary",))


def widths_of(cols):
    return (cols // 2, cols // 4, cols // 8, cols // 8) if cols >= 128 else (cols // 2, cols // 4, cols // 4)


def expand_kernel(off_ref, k_ref, out_ref):
    tile = pl.program_id(0)
    out_ref[...] = jnp.zeros_like(out_ref)
    half_of_lane = lax.broadcasted_iota(jnp.int32, (BS, 2 * BS), 1) // BS
    for local in range(HB):
        rows = pl.ds(local * BS, BS)
        for pair in range(BPR // 2):
            straight = k_ref[rows, pair * 2 * BS : (pair + 1) * 2 * BS].astype(F32)
            swapped = pltpu.roll(straight, BS, 1)
            for half in range(2):
                place = off_ref[tile * HB + local, 2 * pair + half] + (HB + local)
                low = place & 1
                lanes = pl.ds(pl.multiple_of((place >> 1) * (2 * BS), 2 * BS), 2 * BS)
                block = jnp.where(low == half, straight, swapped)
                held = out_ref[0, rows, lanes].astype(F32)
                out_ref[0, rows, lanes] = jnp.where(half_of_lane == low, block, held).astype(BF16)


def expand(stiffness, offsets):
    rows = stiffness.shape[0]
    tiles = rows // TILE
    return pl.pallas_call(
        expand_kernel,
        grid_spec=pltpu.PrefetchScalarGridSpec(
            num_scalar_prefetch=1,
            grid=(tiles,),
            in_specs=[pl.BlockSpec((TILE, BPR * BS), lambda t, off: (t, 0))],
            out_specs=pl.BlockSpec((1, TILE, BAND), lambda t, off: (t, 0, 0)),
        ),
        out_shape=jax.ShapeDtypeStruct((tiles, TILE, BAND), BF16),
        compiler_params=params(),
        name="expand_band",
    )(offsets, stiffness)


def turn_kernel(cols, widths, m_ref, *out_refs):
    eye = (
        lax.broadcasted_iota(jnp.int32, (cols, cols), 0) == lax.broadcasted_iota(jnp.int32, (cols, cols), 1)
    ).astype(BF16)
    for slab in range(m_ref.shape[1] // cols):
        turned = dot(eye, m_ref[:, slab * cols : (slab + 1) * cols], NT).astype(BF16)
        start = 0
        for width, out_ref in zip(widths, out_refs):
            out_ref[slab * width : (slab + 1) * width, :] = turned[start : start + width, :]
            start += width


def turn(modes, cols, widths):
    rows, panel = modes.shape
    slabs = panel // cols
    return pl.pallas_call(
        functools.partial(turn_kernel, cols, widths),
        grid=(rows // TILE,),
        in_specs=[pl.BlockSpec((TILE, panel), lambda t: (t, 0))],
        out_specs=[pl.BlockSpec((slabs * w, TILE), lambda t: (0, t)) for w in widths],
        out_shape=[jax.ShapeDtypeStruct((slabs * w, rows), BF16) for w in widths],
        compiler_params=params(),
        name="turn",
    )(modes)


def own_kernel(tiles, cols, kb_ref, prev_ref, cur_ref, next_ref, left_ref, right_ref, kr_ref, z_ref, zr_ref, g_ref, acc):
    t = pl.program_id(0)
    cur = cur_ref[...]
    before = jnp.where(t == 0, left_ref[...], prev_ref[...])
    after = jnp.where(t == tiles - 1, right_ref[...], next_ref[...])
    z = dot(kb_ref[0, :, :TILE], before)
    z += dot(kb_ref[0, :, TILE : 2 * TILE], cur)
    z += dot(kb_ref[0, :, 2 * TILE :], after)
    z = z.astype(BF16)
    z_ref[...] = z

    @pl.when(t == 0)
    def _():
        acc[...] = jnp.zeros_like(acc)

    acc[...] += dot(cur, z, TN)

    @pl.when(t == tiles - 1)
    def _():
        zr_ref[...] = dot(kr_ref[...], cur).astype(BF16)
        for slab in range(g_ref.shape[0]):
            g_ref[slab] = acc[:, slab * cols : (slab + 1) * cols]


def own_products(band, modes, left, right, reach, cols):
    rows, panel = modes.shape
    tiles = rows // TILE
    slabs = panel // cols
    whole = pl.BlockSpec((TILE, panel), lambda t: (0, 0))
    return pl.pallas_call(
        functools.partial(own_kernel, tiles, cols),
        grid=(tiles,),
        in_specs=[
            pl.BlockSpec((1, TILE, BAND), lambda t: (t, 0, 0)),
            pl.BlockSpec((TILE, panel), lambda t: (jnp.maximum(t - 1, 0), 0)),
            pl.BlockSpec((TILE, panel), lambda t: (t, 0)),
            pl.BlockSpec((TILE, panel), lambda t: (jnp.minimum(t + 1, tiles - 1), 0)),
            whole,
            whole,
            pl.BlockSpec((TILE, TILE), lambda t: (0, 0)),
        ],
        out_specs=[
            pl.BlockSpec((TILE, panel), lambda t: (t, 0)),
            whole,
            pl.BlockSpec((slabs, panel, cols), lambda t: (0, 0, 0)),
        ],
        out_shape=[
            jax.ShapeDtypeStruct((rows, panel), BF16),
            jax.ShapeDtypeStruct((TILE, panel), BF16),
            jax.ShapeDtypeStruct((slabs, panel, cols), F32),
        ],
        scratch_shapes=[pltpu.VMEM((panel, panel), F32)],
        compiler_params=params(),
        name="own_products",
    )(band, modes, modes, modes, left, right, reach)


def pair_kernel(tiles, cols, width, kb_ref, prev_ref, cur_ref, next_ref, xr_ref, m_ref, z_ref, zr_ref, out_ref, own, cross):
    t = pl.program_id(0)
    cur = cur_ref[...]
    before = jnp.where(t == 0, jnp.zeros_like(cur), prev_ref[...])
    after = jnp.where(t == tiles - 1, xr_ref[...], next_ref[...])
    kx = dot(before, kb_ref[0, :, :TILE], NT)
    kx += dot(cur, kb_ref[0, :, TILE : 2 * TILE], NT)
    kx += dot(after, kb_ref[0, :, 2 * TILE :], NT)

    @pl.when(t == 0)
    def _():
        own[...] = jnp.zeros_like(own)
        cross[...] = dot(xr_ref[...], zr_ref[...])

    own[...] += dot(kx.astype(BF16), m_ref[...])
    cross[...] += dot(cur, z_ref[...])

    @pl.when(t == tiles - 1)
    def _():
        slabs = out_ref.shape[1]
        for slab in range(slabs):
            out_ref[0, slab] = cross[:, slab * cols : (slab + 1) * cols]
            for part in range(slabs):
                out_ref[1, slab, part * width : (part + 1) * width, :] = own[
                    slab * width : (slab + 1) * width, part * cols : (part + 1) * cols
                ]


def pair_products(band, turned, turned_right, modes, kphi, reach_kphi, cols, width):
    rows, panel = modes.shape
    tiles = rows // TILE
    slabs = panel // cols
    count = slabs * width
    return pl.pallas_call(
        functools.partial(pair_kernel, tiles, cols, width),
        grid=(tiles,),
        in_specs=[
            pl.BlockSpec((1, TILE, BAND), lambda t: (t, 0, 0)),
            pl.BlockSpec((count, TILE), lambda t: (0, jnp.maximum(t - 1, 0))),
            pl.BlockSpec((count, TILE), lambda t: (0, t)),
            pl.BlockSpec((count, TILE), lambda t: (0, jnp.minimum(t + 1, tiles - 1))),
            pl.BlockSpec((count, TILE), lambda t: (0, 0)),
            pl.BlockSpec((TILE, panel), lambda t: (t, 0)),
            pl.BlockSpec((TILE, panel), lambda t: (t, 0)),
            pl.BlockSpec((TILE, panel), lambda t: (0, 0)),
        ],
        out_specs=pl.BlockSpec((2, slabs, count, cols), lambda t: (0, 0, 0, 0)),
        out_shape=jax.ShapeDtypeStruct((2, slabs, count, cols), F32),
        scratch_shapes=[pltpu.VMEM((count, panel), F32)] * 2,
        compiler_params=params(),
        name="pair_products",
    )(band, turned, turned, turned, turned_right, modes, kphi, reach_kphi)


class Places:
    def __init__(self, mesh):
        self.slabs = mesh.shape["slab"]
        self.panels = mesh.shape["blk"]
        self.group = self.slabs // self.panels
        self.all = [(s, b) for s in range(self.slabs) for b in range(self.panels)]

    def takes(self, slab, b, other):
        return (slab % 2 == 0) == (b < other)

    def send(self, value, pairs):
        flat = [(s * self.panels + b, t * self.panels + c) for (s, b), (t, c) in pairs]
        return lax.ppermute(value, AXES, flat)


def pick(array, index, axis):
    return lax.dynamic_index_in_dim(array, index, axis, keepdims=False)


def halve(places, array, axis, bit, who):
    mine = (lax.axis_index("slab") // bit) % 2
    pairs = [((s, b), (s ^ bit, b)) for s, b in places.all if who(s, b)]
    wire = F32 if bit == 1 else BF16
    return pick(array, mine, axis) + places.send(pick(array, 1 - mine, axis).astype(wire), pairs).astype(F32)


def body(places, modes, stiffness, offsets):
    rows, panel = modes.shape
    group, panels, slabs = places.group, places.panels, places.slabs
    cols = panel // group
    widths = widths_of(cols)
    slab, b = lax.axis_index("slab"), lax.axis_index("blk")
    p, core = slab // group, slab % 2
    everyone = lambda s, c: True

    head = modes[:TILE]
    rights = [
        places.send(
            head,
            [
                ((s + 1, (c - k) % panels), (s, c))
                for s, c in places.all
                if s + 1 < slabs and places.takes(s, c, (c - k) % panels)
            ],
        )
        for k in range(1, panels)
    ]
    chunks = turn(modes, cols, widths)
    arrived = [
        [
            places.send(
                chunk,
                [
                    ((s, (c - k) % panels), (s, c))
                    for s, c in places.all
                    if places.takes(s, c, (c - k) % panels)
                ],
            )
            for chunk in chunks
        ]
        for k in range(1, panels)
    ]
    left = places.send(modes[rows - TILE :], [((s, c), (s + 1, c)) for s, c in places.all if s + 1 < slabs])
    right = places.send(head, [((s + 1, c), (s, c)) for s, c in places.all if s + 1 < slabs])
    band = expand(stiffness, offsets)
    reach = places.send(band[0, :, :TILE], [((s + 1, c), (s, c)) for s, c in places.all if s + 1 < slabs])

    kphi, reach_kphi, square = own_products(band, modes, left, right, reach, cols)
    square = square.reshape(group // 4, 2, 2, panel, cols)
    square = halve(places, square, 2, 1, everyone)
    square = halve(places, square, 1, 2, everyone)
    square = halve(places, square, 0, 4, everyone) if group > 4 else square[0]
    wire = square.astype(BF16)
    for d in range(1, panels):
        pairs = [
            ((s, c), ((s + d * group) % slabs, c)) for s, c in places.all if ((s // group) + d) % panels == c
        ]
        square = square + places.send(wire, pairs).astype(F32)

    own = jnp.zeros((group, cols, cols), F32)
    cross = jnp.zeros((group, cols, cols), F32)
    for k in range(1, panels):
        other = (b - k) % panels
        source = (b + k) % panels
        active = lambda s, c: places.takes(s, c, (c - k) % panels)
        to_me = (core == 0) == (b < other)
        from_same = (core == 0) == (source < b)
        turned_rights = turn(rights[k - 1], cols, widths)
        owns, crosses = [], []
        for chunk, chunk_right, width in zip(arrived[k - 1], turned_rights, widths):
            part = pair_products(band, chunk, chunk_right, modes, kphi, reach_kphi, cols, width)
            part = part.reshape(2, group // 4, 2, 2, group * width, cols)
            part = halve(places, part, 2, 2, active)
            part = halve(places, part, 1, 4, active) if group > 4 else part[:, 0]
            total = pick(part, jnp.where(p == b, 0, 1), 0)
            for d in range(1, panels):
                goal = (p + d) % panels
                pairs = [
                    ((s, c), ((s + d * group) % slabs, c))
                    for s, c in places.all
                    if active(s, c) and ((s // group) + d) % panels in (c, (c - k) % panels)
                ]
                total = total + places.send(
                    pick(part, jnp.where(goal == b, 0, 1), 0).astype(BF16), pairs
                ).astype(F32)
            stay, leave = pick(total, core, 0), pick(total, 1 - core, 0)
            pairs_core, pairs_same = [], []
            for s, c in places.all:
                if active(s, c):
                    if s // group == (c - k) % panels:
                        pairs_core.append(((s, c), (s ^ 1, c)))
                    if s // group == c:
                        pairs_core.append(((s, c), (s ^ 1, (c - k) % panels)))
                        pairs_same.append(((s, c), (s, (c - k) % panels)))
            got_core = places.send(leave, pairs_core)
            got_same = places.send(stay, pairs_same)
            owns.append(jnp.where(to_me, stay, got_core).reshape(group, width, cols))
            crosses.append(jnp.where(from_same, got_same, got_core).reshape(group, width, cols))
        own = own + jnp.where(p == other, jnp.concatenate(owns, 1), 0)
        cross = cross + jnp.where(p == source, jnp.concatenate(crosses, 1), 0)

    off = (jnp.swapaxes(own, 1, 2) + cross).reshape(panel, cols)
    return jnp.where(p == b, square, off)


def solution(mesh):
    in_specs = (P("slab", "blk"), P("slab", None), P("slab", None))
    out_specs = P("blk", "slab")
    return jax.shard_map(
        functools.partial(body, Places(mesh)), mesh=mesh, in_specs=in_specs, out_specs=out_specs, check_vma=False
    )
```

```python
import functools
import itertools

import jax
import jax.numpy as jnp
from jax import lax
from jax.experimental import pallas as pl
from jax.experimental.pallas import tpu as pltpu
from jax.sharding import PartitionSpec as P

BS = 64
HB = 4
BPR = 8
TILE = HB * BS
BAND = 3 * TILE
STEP = 4
AXES = ("slab", "blk")
F32 = jnp.float32
BF16 = jnp.bfloat16
NT = (((1,), (1,)), ((), ()))
TN = (((0,), (0,)), ((), ()))
VMEM_LIMIT = 56 * 1024 * 1024


def dot(a, b, dims=(((1,), (0,)), ((), ()))):
    return lax.dot_general(a, b, dims, preferred_element_type=F32)


def params():
    return pltpu.CompilerParams(vmem_limit_bytes=VMEM_LIMIT, dimension_semantics=("arbitrary",))


def plan_of(cols):
    if cols == 128:
        return (16, 32, 32, 48), ((0, 1), (2,), (3,))
    return (cols // 4,) * 4, ((0, 1), (2,), (3,))


def expand_kernel(count, off_ref, k_ref, out_ref, first_ref, held):
    step = pl.program_id(0)
    lower = lax.broadcasted_iota(jnp.int32, (BS, 2 * BS), 1) < BS
    held[...] = jnp.zeros_like(held)
    for row in range(count * HB):
        for pair in range(BPR // 2):
            straight = k_ref[row * BS : (row + 1) * BS, pair * 2 * BS : (pair + 1) * 2 * BS]
            swapped = pltpu.roll(straight.astype(F32), BS, 1).astype(BF16)
            for half in range(2):
                place = off_ref[step * (count * HB) + row, 2 * pair + half] + (HB + row % HB)
                held[row, place] = jnp.where((place & 1) == half, straight, swapped)
    for row in range(count * HB):
        rows = slice(row % HB * BS, (row % HB + 1) * BS)
        for pair in range(3 * HB // 2):
            out_ref[row // HB, rows, pair * 2 * BS : (pair + 1) * 2 * BS] = jnp.where(
                lower, held[row, 2 * pair], held[row, 2 * pair + 1]
            )

    @pl.when(step == 0)
    def _():
        first_ref[...] = out_ref[0, :, :TILE]


def expand(stiffness, offsets):
    rows = stiffness.shape[0]
    tiles = rows // TILE
    count = STEP
    return pl.pallas_call(
        functools.partial(expand_kernel, count),
        grid_spec=pltpu.PrefetchScalarGridSpec(
            num_scalar_prefetch=1,
            grid=(tiles // count,),
            in_specs=[pl.BlockSpec((count * TILE, BPR * BS), lambda t, off: (t, 0))],
            out_specs=[
                pl.BlockSpec((count, TILE, BAND), lambda t, off: (t, 0, 0)),
                pl.BlockSpec((TILE, TILE), lambda t, off: (0, 0)),
            ],
            scratch_shapes=[pltpu.VMEM((count * HB, 3 * HB, BS, 2 * BS), BF16)],
        ),
        out_shape=[jax.ShapeDtypeStruct((tiles, TILE, BAND), BF16), jax.ShapeDtypeStruct((TILE, TILE), BF16)],
        compiler_params=params(),
        name="expand_band",
    )(offsets, stiffness)


def copy_kernel(at_ref, from_ref, to_ref):
    to_ref[...] = from_ref[...]


def take_tile(modes, at):
    block = (TILE, modes.shape[1])
    return pl.pallas_call(
        copy_kernel,
        grid_spec=pltpu.PrefetchScalarGridSpec(
            num_scalar_prefetch=1,
            grid=(1,),
            in_specs=[pl.BlockSpec(block, lambda t, at: (at[0], 0))],
            out_specs=pl.BlockSpec(block, lambda t, at: (0, 0)),
        ),
        out_shape=jax.ShapeDtypeStruct(block, modes.dtype),
        compiler_params=params(),
        name="take_tile",
    )(at, modes)


def fold_kernel(at_ref, keep_ref, came_keep_ref, give_ref, came_give_ref, kept_ref, given_ref):
    kept_ref[...] = keep_ref[...] + came_keep_ref[...].astype(F32)
    given_ref[...] = (give_ref[...] + came_give_ref[...].astype(F32)).astype(given_ref.dtype)


def fold(at, held, came, wire):
    count, _, rows, cols = held.shape
    block = (count, pl.squeezed, rows, cols)
    keep = pl.BlockSpec(block, lambda t, at: (0, at[0], 0, 0))
    give = pl.BlockSpec(block, lambda t, at: (0, 1 - at[0], 0, 0))
    out = pl.BlockSpec((count, rows, cols), lambda t, at: (0, 0, 0))
    return pl.pallas_call(
        fold_kernel,
        grid_spec=pltpu.PrefetchScalarGridSpec(
            num_scalar_prefetch=1, grid=(1,), in_specs=[keep, keep, give, give], out_specs=[out, out]
        ),
        out_shape=[jax.ShapeDtypeStruct((count, rows, cols), kind) for kind in (F32, wire)],
        compiler_params=params(),
        name="fold",
    )(at, held, came, held, came)


def deal_out_kernel(at_ref, mine_ref, came_ref, out_ref):
    panel = pl.program_id(0)
    total = mine_ref[0] + came_ref[0].astype(F32)
    ours = jnp.logical_or(panel == at_ref[0], panel == at_ref[1])
    out_ref[0] = jnp.where(ours, total, 0).astype(BF16)


def deal_out_sums(at, mine, came, panels):
    block = (1, *mine.shape[1:])
    part = pl.BlockSpec(block, lambda panel, at: (jnp.where(panel == at[0], 0, 1), 0, 0, 0))
    return pl.pallas_call(
        deal_out_kernel,
        grid_spec=pltpu.PrefetchScalarGridSpec(
            num_scalar_prefetch=1,
            grid=(panels,),
            in_specs=[part, part],
            out_specs=pl.BlockSpec(block, lambda panel, at: (panel, 0, 0, 0)),
        ),
        out_shape=jax.ShapeDtypeStruct((panels, *mine.shape[1:]), BF16),
        compiler_params=params(),
        name="deal_out_sums",
    )(at, mine, came)


def gather_up_kernel(came_ref, out_ref):
    out_ref[...] = jnp.sum(came_ref[...].astype(F32), axis=0)


def gather_up_sums(came):
    return pl.pallas_call(
        gather_up_kernel,
        out_shape=jax.ShapeDtypeStruct(came.shape[1:], F32),
        compiler_params=pltpu.CompilerParams(vmem_limit_bytes=VMEM_LIMIT),
        name="gather_up_sums",
    )(came)


def turn_kernel(cols, widths, at_ref, m_ref, *out_refs):
    for slab in range(m_ref.shape[1] // cols):
        turned = m_ref[:, slab * cols : (slab + 1) * cols].T
        start = 0
        for width, out_ref in zip(widths, out_refs):
            out_ref[slab * width : (slab + 1) * width, :] = turned[start : start + width, :]
            start += width


def turn(modes, rows, at, cols, widths):
    panel = modes.shape[1]
    slabs = panel // cols
    block = min(rows, STEP * TILE)
    steps = rows // block
    return pl.pallas_call(
        functools.partial(turn_kernel, cols, widths),
        grid_spec=pltpu.PrefetchScalarGridSpec(
            num_scalar_prefetch=1,
            grid=(steps,),
            in_specs=[pl.BlockSpec((block, panel), lambda t, at: (at[0] * steps + t, 0))],
            out_specs=[pl.BlockSpec((slabs * w, block), lambda t, at: (0, t)) for w in widths],
        ),
        out_shape=[jax.ShapeDtypeStruct((slabs * w, rows), BF16) for w in widths],
        compiler_params=params(),
        name="turn",
    )(at, modes)


def deal(core, both, mine_ref, theirs_ref, index):
    even, odd = both
    mine_ref[index] = jnp.where(core == 0, even, odd)
    theirs_ref[index] = jnp.where(core == 0, odd, even).astype(theirs_ref.dtype)


def kphi_kernel(steps, kb_ref, prev_ref, cur_ref, next_ref, left_ref, right_ref, z_ref):
    t = pl.program_id(0)
    before = jnp.where(t == 0, left_ref[...], prev_ref[...])
    after = jnp.where(t == steps - 1, right_ref[...], next_ref[...])
    window = jnp.concatenate([before, cur_ref[...], after], axis=0)
    for tile in range(STEP):
        rows = slice(tile * TILE, (tile + 1) * TILE)
        z_ref[rows, :] = dot(kb_ref[tile], window[tile * TILE : tile * TILE + BAND]).astype(BF16)


def own_kphi(band, modes, left, right):
    rows, panel = modes.shape
    tiles = rows // TILE
    steps = tiles // STEP
    whole = pl.BlockSpec((TILE, panel), lambda t: (0, 0))
    return pl.pallas_call(
        functools.partial(kphi_kernel, steps),
        grid=(steps,),
        in_specs=[
            pl.BlockSpec((STEP, TILE, BAND), lambda t: (t, 0, 0)),
            pl.BlockSpec((TILE, panel), lambda t: (jnp.maximum(t * STEP - 1, 0), 0)),
            pl.BlockSpec((STEP * TILE, panel), lambda t: (t, 0)),
            pl.BlockSpec((TILE, panel), lambda t: (jnp.minimum((t + 1) * STEP, tiles - 1), 0)),
            whole,
            whole,
        ],
        out_specs=pl.BlockSpec((STEP * TILE, panel), lambda t: (t, 0)),
        out_shape=jax.ShapeDtypeStruct((rows, panel), BF16),
        compiler_params=params(),
        name="own_kphi",
    )(band, modes, modes, modes, left, right)


def square_kernel(steps, cols, at_ref, m_ref, z_ref, mine_ref, theirs_ref, acc):
    t = pl.program_id(0)

    @pl.when(t == 0)
    def _():
        acc[...] = jnp.zeros_like(acc)

    acc[...] += dot(m_ref[...], z_ref[...], TN)

    @pl.when(t == steps - 1)
    def _():
        for pair in range(mine_ref.shape[0]):
            first = 2 * pair * cols
            deal(at_ref[0], (acc[:, first : first + cols], acc[:, first + cols : first + 2 * cols]), mine_ref, theirs_ref, pair)


def own_square(core, modes, kphi, cols):
    rows, panel = modes.shape
    steps = rows // TILE // STEP
    pairs = panel // cols // 2
    here = pl.BlockSpec((STEP * TILE, panel), lambda t, at: (t, 0))
    dealt = pl.BlockSpec((pairs, panel, cols), lambda t, at: (0, 0, 0))
    return pl.pallas_call(
        functools.partial(square_kernel, steps, cols),
        grid_spec=pltpu.PrefetchScalarGridSpec(
            num_scalar_prefetch=1,
            grid=(steps,),
            in_specs=[here, here],
            out_specs=[dealt, dealt],
            scratch_shapes=[pltpu.VMEM((panel, panel), F32)],
        ),
        out_shape=[jax.ShapeDtypeStruct((pairs, panel, cols), kind) for kind in (F32, BF16)],
        compiler_params=params(),
        name="own_square",
    )(core, modes, kphi)


def pair_kernel(steps, cols, widths, at_ref, kb_ref, *refs):
    pieces = len(widths)
    prevs, curs, nexts, rights = (refs[i * pieces : (i + 1) * pieces] for i in range(4))
    m_ref, z_ref, mid_ref, reach_ref, last_ref, mine_ref, theirs_ref, own, cross = refs[4 * pieces :]
    t = pl.program_id(0)
    join = lambda parts: jnp.concatenate([part[...] for part in parts], axis=0)
    cur, right = join(curs), join(rights)
    before = join(prevs)
    before = jnp.where(t == 0, jnp.zeros_like(before), before)
    after = jnp.where(t == steps - 1, right, join(nexts))
    window = jnp.concatenate([before, cur, after], axis=1)
    kx = [dot(window[:, tile * TILE : tile * TILE + BAND], kb_ref[tile], NT).astype(BF16) for tile in range(STEP)]

    @pl.when(t == 0)
    def _():
        own[...] = jnp.zeros_like(own)
        edge = jnp.where(at_ref[1] == 0, mid_ref[0], reach_ref[...])
        cross[...] = dot(right, dot(edge, last_ref[...]).astype(BF16))

    own[...] += dot(jnp.concatenate(kx, axis=1), m_ref[...])
    cross[...] += dot(cur, z_ref[...])

    @pl.when(t == steps - 1)
    def _():
        pairs = mine_ref.shape[1]
        for piece, slab in itertools.product(range(pieces), range(2 * pairs)):
            width = widths[piece]
            lead = 2 * pairs * sum(widths[:piece])
            rows = lambda where: slice(lead + where * width, lead + (where + 1) * width)
            lanes = lambda where: slice(where * cols, (where + 1) * cols)
            start = slab * sum(widths) + sum(widths[:piece])
            to = slice(start, start + width)
            for pair in range(pairs):
                ends = (2 * pair, 2 * pair + 1)
                deal(at_ref[0], [cross[rows(slab), lanes(end)] for end in ends], mine_ref, theirs_ref, (0, pair, to))
                deal(at_ref[0], [own[rows(end), lanes(slab)] for end in ends], mine_ref, theirs_ref, (1, pair, to))


def pair_products(at, band, turned, turned_right, modes, kphi, reach, cols, widths):
    rows, panel = modes.shape
    tiles = rows // TILE // 2
    steps = tiles // STEP
    slabs = panel // cols
    some = [slabs * width for width in widths]
    count = sum(some)
    dealt = pl.BlockSpec((2, slabs // 2, count, cols), lambda t, at: (0, 0, 0, 0))
    here = pl.BlockSpec((STEP * TILE, panel), lambda t, at: (at[1] * steps + t, 0))
    return pl.pallas_call(
        functools.partial(pair_kernel, steps, cols, widths),
        grid_spec=pltpu.PrefetchScalarGridSpec(
            num_scalar_prefetch=1,
            grid=(steps,),
            in_specs=[
                pl.BlockSpec((STEP, TILE, BAND), lambda t, at: (at[1] * steps + t, 0, 0)),
                *[pl.BlockSpec((n, TILE), lambda t, at: (0, jnp.maximum(t * STEP - 1, 0))) for n in some],
                *[pl.BlockSpec((n, STEP * TILE), lambda t, at: (0, t)) for n in some],
                *[pl.BlockSpec((n, TILE), lambda t, at: (0, jnp.minimum((t + 1) * STEP, tiles - 1))) for n in some],
                *[pl.BlockSpec((n, TILE), lambda t, at: (0, 0)) for n in some],
                here,
                here,
                pl.BlockSpec((1, TILE, TILE), lambda t, at: (tiles, 0, 0)),
                pl.BlockSpec((TILE, TILE), lambda t, at: (0, 0)),
                pl.BlockSpec((TILE, panel), lambda t, at: (at[1] * tiles + tiles - 1, 0)),
            ],
            out_specs=[dealt, dealt],
            scratch_shapes=[pltpu.VMEM((count, panel), F32)] * 2,
        ),
        out_shape=[jax.ShapeDtypeStruct((2, slabs // 2, count, cols), kind) for kind in (F32, BF16)],
        compiler_params=params(),
        name="pair_products",
    )(at, band, *turned, *turned, *turned, *turned_right, modes, kphi, band, reach, modes)


class Places:
    def __init__(self, mesh):
        self.slabs = mesh.shape["slab"]
        self.panels = mesh.shape["blk"]
        self.group = self.slabs // self.panels
        self.all = [(s, b) for s in range(self.slabs) for b in range(self.panels)]

    def send(self, value, pairs):
        flat = [(s * self.panels + b, t * self.panels + c) for (s, b), (t, c) in pairs]
        return lax.ppermute(value, AXES, flat)

    def across(self, value, bit):
        return self.send(value, [((s, b), (s ^ bit, b)) for s, b in self.all])


def pick(array, index, axis=0):
    return lax.dynamic_index_in_dim(array, index, axis, keepdims=False)


def tie(value, *others):
    return lax.optimization_barrier((value, others))[0]


def body(places, modes, stiffness, offsets):
    rows, panel = modes.shape
    group, panels, slabs = places.group, places.panels, places.slabs
    cols = panel // group
    widths, groups = plan_of(cols)
    half = rows // 2
    slab, b = lax.axis_index("slab"), lax.axis_index("blk")
    p, core = slab // group, slab % 2
    one = lambda *values: jnp.stack([jnp.asarray(v, jnp.int32) for v in values])
    core_at, x_at, z_at, panel_at = one(core), one(slab // 2 % 2), one(slab // 4 % 2), one(jnp.where(p == b, 0, 1))
    zl = group // 4

    rights, ready = [], []
    for k in range(1, panels):
        pairs = []
        for s, c in places.all:
            other = (c - k) % panels
            if c < other:
                pairs.append(((s, other), (s, c)))
            elif s + 1 < slabs:
                pairs.append(((s + 1, other), (s, c)))
        tile = take_tile(modes, one(jnp.where((b + k) % panels < b, half // TILE, 0)))
        rights.append(places.send(tile, pairs))
    for k in range(1, panels):
        ready.append(turn(modes, half, one(jnp.where((b + k) % panels < b, 0, 1)), cols, widths))
    to_right = [((s, c), (s + 1, c)) for s, c in places.all if s + 1 < slabs]
    to_left = [(there, here) for here, there in to_right]
    left = places.send(tie(modes[rows - TILE :], ready), to_right)
    right = places.send(tie(modes[:TILE], ready), to_left)
    stiffness, ready = lax.optimization_barrier((stiffness, ready))
    band, first_band = expand(stiffness, offsets)
    reach = places.send(first_band, to_left)

    own = jnp.zeros((group, cols, cols), F32)
    cross = jnp.zeros((group, cols, cols), F32)
    for k in range(1, panels):
        other = (b - k) % panels
        source = (b + k) % panels
        at = one(core, jnp.where(b < other, 0, 1))
        there = [((s, c), (s, (c + k) % panels)) for s, c in places.all]
        same_core = [list(range(first, slabs, 2)) for first in range(2)]
        pieces = ready[k - 1]

        arrived = [places.send(pieces[0], there)]
        arrived.append(places.send(tie(pieces[1], arrived[0], left, right, rights, band), there))
        if k == 1:
            kphi = own_kphi(tie(band, rights, arrived[0]), modes, left, right)
        turned_rights = turn(rights[k - 1], TILE, one(0), cols, widths)
        arrived.append(places.send(tie(pieces[2], kphi), there))
        if k == 1:
            square = own_square(core_at, modes, tie(kphi, reach), cols)
        for piece in pieces[3:]:
            arrived.append(places.send(tie(piece, arrived[len(arrived) - 2]), there))

        def multiply(members, *gates):
            took = [tie(arrived[piece], *gates) for piece in members]
            tails = [turned_rights[piece] for piece in members]
            return pair_products(at, band, took, tails, modes, kphi, reach, cols, [widths[piece] for piece in members])

        def over_core(mine, theirs):
            return deal_out_sums(one(b, other), mine, places.across(theirs, 1), panels)

        def deal_out(parts):
            parts = parts.reshape(slabs // 2, *parts.shape[2:])
            return lax.all_to_all(parts, "slab", 0, 0, axis_index_groups=same_core)

        def gather_up(came, *gates):
            return gather_up_sums(tie(came, *gates)).reshape(group, -1, cols)

        def square_over(kept, given, bit, where, wire=BF16):
            shape = (-1, 2, *kept.shape[-2:])
            return fold(where, kept.reshape(shape), places.across(given, bit).reshape(shape), wire)

        def square_over_panels(kept, given):
            total = kept[0] + places.across(given, 4)[0].astype(F32) if group > 4 else kept[0]
            wire = total.astype(BF16)
            for d in range(1, panels):
                goal = lambda s: (s + d * group) % slabs
                pairs = [((s, c), (goal(s), c)) for s, c in places.all if goal(s) // group == c]
                total = total + places.send(wire, pairs).astype(F32)
            return total

        mine, theirs = multiply(groups[0], square[1])
        if k == 1:
            square_sum = square_over(*square, 1, x_at)
        first = over_core(mine, tie(theirs, arrived[groups[1][0]]))
        mine, theirs = multiply(groups[1], first, square_sum if k == 1 else ())
        first = gather_up(deal_out(first))
        second = over_core(mine, theirs)
        if k == 1:
            kept, given = square_sum
            square_sum = square_over(kept, given, 2, z_at) if group > 4 else [kept + places.across(given, 2).astype(F32)] * 2
        mine, theirs = multiply(groups[2], second)
        second = deal_out(second)
        third = deal_out(over_core(mine, tie(theirs, first, square_sum if k == 1 else ())))
        if k == 1:
            square_sum = square_over_panels(*square_sum)
        second = gather_up(second)
        third = gather_up(third, second)
        if k == 1:
            total_square = square_sum
        pairs = [((s, c), (s, (c - k) % panels)) for s, c in places.all if s // group == c]
        early = jnp.concatenate((first, second), 1)
        early_came = places.send(early, pairs)
        late = tie(third, early_came)
        came = jnp.concatenate([early_came, places.send(late, pairs)], 1)
        own = own + jnp.where(p == other, jnp.concatenate([early, late], 1), 0)
        cross = cross + jnp.where(p == source, came, 0)

    off = (jnp.swapaxes(own, 1, 2) + cross).reshape(panel, cols)
    return jnp.where(p == b, total_square, off)


def solution(mesh):
    in_specs = (P("slab", "blk"), P("slab", None), P("slab", None))
    out_specs = P("blk", "slab")
    return jax.shard_map(
        functools.partial(body, Places(mesh)), mesh=mesh, in_specs=in_specs, out_specs=out_specs, check_vma=False
    )
```

```python
import functools
import itertools

import jax
import jax.numpy as jnp
from jax import lax
from jax.experimental import pallas as pl
from jax.experimental.pallas import tpu as pltpu
from jax.sharding import PartitionSpec as P

BS = 64
HB = 4
BPR = 8
TILE = HB * BS
BAND = 3 * TILE
STEP = 4
AXES = ("slab", "blk")
F32 = jnp.float32
BF16 = jnp.bfloat16
NT = (((1,), (1,)), ((), ()))
TN = (((0,), (0,)), ((), ()))
VMEM_LIMIT = 62 * 1024 * 1024


def dot(a, b, dims=(((1,), (0,)), ((), ()))):
    return lax.dot_general(a, b, dims, preferred_element_type=F32)


def params():
    return pltpu.CompilerParams(vmem_limit_bytes=VMEM_LIMIT, dimension_semantics=("arbitrary",))


def plan_of(cols):
    if cols == 128:
        return (16, 32, 32, 48), ((0, 1), (2,), (3,))
    return (cols // 4,) * 4, ((0, 1), (2,), (3,))


def expand_kernel(count, off_ref, k_ref, out_ref, first_ref, held):
    step = pl.program_id(0)
    lower = lax.broadcasted_iota(jnp.int32, (BS, 2 * BS), 1) < BS
    held[...] = jnp.zeros_like(held)
    for row in range(count * HB):
        for pair in range(BPR // 2):
            straight = k_ref[row * BS : (row + 1) * BS, pair * 2 * BS : (pair + 1) * 2 * BS]
            swapped = pltpu.roll(straight.astype(F32), BS, 1).astype(BF16)
            for half in range(2):
                place = off_ref[step * (count * HB) + row, 2 * pair + half] + (HB + row % HB)
                held[row, place] = jnp.where((place & 1) == half, straight, swapped)
    for row in range(count * HB):
        rows = slice(row % HB * BS, (row % HB + 1) * BS)
        for pair in range(3 * HB // 2):
            out_ref[row // HB, rows, pair * 2 * BS : (pair + 1) * 2 * BS] = jnp.where(
                lower, held[row, 2 * pair], held[row, 2 * pair + 1]
            )

    @pl.when(step == 0)
    def _():
        first_ref[...] = out_ref[0, :, :TILE]


def expand(stiffness, offsets):
    rows = stiffness.shape[0]
    tiles = rows // TILE
    count = STEP
    return pl.pallas_call(
        functools.partial(expand_kernel, count),
        grid_spec=pltpu.PrefetchScalarGridSpec(
            num_scalar_prefetch=1,
            grid=(tiles // count,),
            in_specs=[pl.BlockSpec((count * TILE, BPR * BS), lambda t, off: (t, 0))],
            out_specs=[
                pl.BlockSpec((count, TILE, BAND), lambda t, off: (t, 0, 0)),
                pl.BlockSpec((TILE, TILE), lambda t, off: (0, 0)),
            ],
            scratch_shapes=[pltpu.VMEM((count * HB, 3 * HB, BS, 2 * BS), BF16)],
        ),
        out_shape=[jax.ShapeDtypeStruct((tiles, TILE, BAND), BF16), jax.ShapeDtypeStruct((TILE, TILE), BF16)],
        compiler_params=params(),
        name="expand_band",
    )(offsets, stiffness)


def copy_kernel(at_ref, from_ref, to_ref):
    to_ref[...] = from_ref[...]


def take_tile(modes, at):
    block = (TILE, modes.shape[1])
    return pl.pallas_call(
        copy_kernel,
        grid_spec=pltpu.PrefetchScalarGridSpec(
            num_scalar_prefetch=1,
            grid=(1,),
            in_specs=[pl.BlockSpec(block, lambda t, at: (at[0], 0))],
            out_specs=pl.BlockSpec(block, lambda t, at: (0, 0)),
        ),
        out_shape=jax.ShapeDtypeStruct(block, modes.dtype),
        compiler_params=params(),
        name="take_tile",
    )(at, modes)


def fold_kernel(at_ref, keep_ref, came_keep_ref, give_ref, came_give_ref, kept_ref, given_ref):
    kept_ref[...] = keep_ref[...] + came_keep_ref[...].astype(F32)
    given_ref[...] = (give_ref[...] + came_give_ref[...].astype(F32)).astype(given_ref.dtype)


def fold(at, held, came, wire):
    count, _, rows, cols = held.shape
    block = (count, pl.squeezed, rows, cols)
    keep = pl.BlockSpec(block, lambda t, at: (0, at[0], 0, 0))
    give = pl.BlockSpec(block, lambda t, at: (0, 1 - at[0], 0, 0))
    out = pl.BlockSpec((count, rows, cols), lambda t, at: (0, 0, 0))
    return pl.pallas_call(
        fold_kernel,
        grid_spec=pltpu.PrefetchScalarGridSpec(
            num_scalar_prefetch=1, grid=(1,), in_specs=[keep, keep, give, give], out_specs=[out, out]
        ),
        out_shape=[jax.ShapeDtypeStruct((count, rows, cols), kind) for kind in (F32, wire)],
        compiler_params=params(),
        name="fold",
    )(at, held, came, held, came)


def deal_out_kernel(at_ref, mine_ref, came_ref, out_ref):
    panel = pl.program_id(0)
    total = mine_ref[0] + came_ref[0].astype(F32)
    ours = jnp.logical_or(panel == at_ref[0], panel == at_ref[1])
    out_ref[0] = jnp.where(ours, total, 0).astype(BF16)


def deal_out_sums(at, mine, came, panels):
    block = (1, *mine.shape[1:])
    part = pl.BlockSpec(block, lambda panel, at: (jnp.where(panel == at[0], 0, 1), 0, 0, 0))
    return pl.pallas_call(
        deal_out_kernel,
        grid_spec=pltpu.PrefetchScalarGridSpec(
            num_scalar_prefetch=1,
            grid=(panels,),
            in_specs=[part, part],
            out_specs=pl.BlockSpec(block, lambda panel, at: (panel, 0, 0, 0)),
        ),
        out_shape=jax.ShapeDtypeStruct((panels, *mine.shape[1:]), BF16),
        compiler_params=params(),
        name="deal_out_sums",
    )(at, mine, came)


def gather_up_kernel(came_ref, out_ref):
    out_ref[...] = jnp.sum(came_ref[...].astype(F32), axis=0)


def gather_up_sums(came):
    return pl.pallas_call(
        gather_up_kernel,
        out_shape=jax.ShapeDtypeStruct(came.shape[1:], F32),
        compiler_params=pltpu.CompilerParams(vmem_limit_bytes=VMEM_LIMIT),
        name="gather_up_sums",
    )(came)


def turn_kernel(cols, widths, at_ref, m_ref, *out_refs):
    for slab in range(m_ref.shape[1] // cols):
        turned = m_ref[:, slab * cols : (slab + 1) * cols].T
        start = 0
        for width, out_ref in zip(widths, out_refs):
            out_ref[slab * width : (slab + 1) * width, :] = turned[start : start + width, :]
            start += width


def turn(modes, rows, at, cols, widths):
    panel = modes.shape[1]
    slabs = panel // cols
    block = min(rows, STEP * TILE)
    steps = rows // block
    return pl.pallas_call(
        functools.partial(turn_kernel, cols, widths),
        grid_spec=pltpu.PrefetchScalarGridSpec(
            num_scalar_prefetch=1,
            grid=(steps,),
            in_specs=[pl.BlockSpec((block, panel), lambda t, at: (at[0] * steps + t, 0))],
            out_specs=[pl.BlockSpec((slabs * w, block), lambda t, at: (0, t)) for w in widths],
        ),
        out_shape=[jax.ShapeDtypeStruct((slabs * w, rows), BF16) for w in widths],
        compiler_params=params(),
        name="turn",
    )(at, modes)


def deal(core, both, mine_ref, theirs_ref, index):
    even, odd = both
    mine_ref[index] = jnp.where(core == 0, even, odd)
    theirs_ref[index] = jnp.where(core == 0, odd, even).astype(theirs_ref.dtype)


def kphi_kernel(steps, kb_ref, prev_ref, cur_ref, next_ref, left_ref, right_ref, z_ref):
    t = pl.program_id(0)
    before = jnp.where(t == 0, left_ref[...], prev_ref[...])
    after = jnp.where(t == steps - 1, right_ref[...], next_ref[...])
    window = jnp.concatenate([before, cur_ref[...], after], axis=0)
    for tile in range(STEP):
        rows = slice(tile * TILE, (tile + 1) * TILE)
        z_ref[rows, :] = dot(kb_ref[tile], window[tile * TILE : tile * TILE + BAND]).astype(BF16)


def own_kphi(band, modes, left, right):
    rows, panel = modes.shape
    tiles = rows // TILE
    steps = tiles // STEP
    whole = pl.BlockSpec((TILE, panel), lambda t: (0, 0))
    return pl.pallas_call(
        functools.partial(kphi_kernel, steps),
        grid=(steps,),
        in_specs=[
            pl.BlockSpec((STEP, TILE, BAND), lambda t: (t, 0, 0)),
            pl.BlockSpec((TILE, panel), lambda t: (jnp.maximum(t * STEP - 1, 0), 0)),
            pl.BlockSpec((STEP * TILE, panel), lambda t: (t, 0)),
            pl.BlockSpec((TILE, panel), lambda t: (jnp.minimum((t + 1) * STEP, tiles - 1), 0)),
            whole,
            whole,
        ],
        out_specs=pl.BlockSpec((STEP * TILE, panel), lambda t: (t, 0)),
        out_shape=jax.ShapeDtypeStruct((rows, panel), BF16),
        compiler_params=params(),
        name="own_kphi",
    )(band, modes, modes, modes, left, right)


def square_kernel(steps, cols, at_ref, m_ref, z_ref, mine_ref, theirs_ref, acc):
    t = pl.program_id(0)

    @pl.when(t == 0)
    def _():
        acc[...] = jnp.zeros_like(acc)

    acc[...] += dot(m_ref[...], z_ref[...], TN)

    @pl.when(t == steps - 1)
    def _():
        for pair in range(mine_ref.shape[0]):
            first = 2 * pair * cols
            deal(at_ref[0], (acc[:, first : first + cols], acc[:, first + cols : first + 2 * cols]), mine_ref, theirs_ref, pair)


def own_square(core, modes, kphi, cols):
    rows, panel = modes.shape
    steps = rows // TILE // STEP
    pairs = panel // cols // 2
    here = pl.BlockSpec((STEP * TILE, panel), lambda t, at: (t, 0))
    dealt = pl.BlockSpec((pairs, panel, cols), lambda t, at: (0, 0, 0))
    return pl.pallas_call(
        functools.partial(square_kernel, steps, cols),
        grid_spec=pltpu.PrefetchScalarGridSpec(
            num_scalar_prefetch=1,
            grid=(steps,),
            in_specs=[here, here],
            out_specs=[dealt, dealt],
            scratch_shapes=[pltpu.VMEM((panel, panel), F32)],
        ),
        out_shape=[jax.ShapeDtypeStruct((pairs, panel, cols), kind) for kind in (F32, BF16)],
        compiler_params=params(),
        name="own_square",
    )(core, modes, kphi)


def pair_kernel(steps, cols, widths, at_ref, kb_ref, *refs):
    pieces = len(widths)
    prevs, curs, nexts, rights = (refs[i * pieces : (i + 1) * pieces] for i in range(4))
    m_ref, z_ref, mid_ref, reach_ref, last_ref, mine_ref, theirs_ref, own, cross = refs[4 * pieces :]
    t = pl.program_id(0)
    join = lambda parts: jnp.concatenate([part[...] for part in parts], axis=0)
    cur, right = join(curs), join(rights)
    before = join(prevs)
    before = jnp.where(t == 0, jnp.zeros_like(before), before)
    after = jnp.where(t == steps - 1, right, join(nexts))
    window = jnp.concatenate([before, cur, after], axis=1)
    kx = [dot(window[:, tile * TILE : tile * TILE + BAND], kb_ref[tile], NT).astype(BF16) for tile in range(STEP)]

    @pl.when(t == 0)
    def _():
        own[...] = jnp.zeros_like(own)
        edge = jnp.where(at_ref[1] == 0, mid_ref[0], reach_ref[...])
        cross[...] = dot(right, dot(edge, last_ref[...]).astype(BF16))

    own[...] += dot(jnp.concatenate(kx, axis=1), m_ref[...])
    cross[...] += dot(cur, z_ref[...])

    @pl.when(t == steps - 1)
    def _():
        pairs = mine_ref.shape[1]
        for piece, slab in itertools.product(range(pieces), range(2 * pairs)):
            width = widths[piece]
            lead = 2 * pairs * sum(widths[:piece])
            rows = lambda where: slice(lead + where * width, lead + (where + 1) * width)
            lanes = lambda where: slice(where * cols, (where + 1) * cols)
            start = slab * sum(widths) + sum(widths[:piece])
            to = slice(start, start + width)
            for pair in range(pairs):
                ends = (2 * pair, 2 * pair + 1)
                deal(at_ref[0], [cross[rows(slab), lanes(end)] for end in ends], mine_ref, theirs_ref, (0, pair, to))
                deal(at_ref[0], [own[rows(end), lanes(slab)] for end in ends], mine_ref, theirs_ref, (1, pair, to))


def pair_products(at, band, turned, turned_right, modes, kphi, reach, cols, widths):
    rows, panel = modes.shape
    tiles = rows // TILE // 2
    steps = tiles // STEP
    slabs = panel // cols
    some = [slabs * width for width in widths]
    count = sum(some)
    dealt = pl.BlockSpec((2, slabs // 2, count, cols), lambda t, at: (0, 0, 0, 0))
    here = pl.BlockSpec((STEP * TILE, panel), lambda t, at: (at[1] * steps + t, 0))
    return pl.pallas_call(
        functools.partial(pair_kernel, steps, cols, widths),
        grid_spec=pltpu.PrefetchScalarGridSpec(
            num_scalar_prefetch=1,
            grid=(steps,),
            in_specs=[
                pl.BlockSpec((STEP, TILE, BAND), lambda t, at: (at[1] * steps + t, 0, 0)),
                *[pl.BlockSpec((n, TILE), lambda t, at: (0, jnp.maximum(t * STEP - 1, 0))) for n in some],
                *[pl.BlockSpec((n, STEP * TILE), lambda t, at: (0, t)) for n in some],
                *[pl.BlockSpec((n, TILE), lambda t, at: (0, jnp.minimum((t + 1) * STEP, tiles - 1))) for n in some],
                *[pl.BlockSpec((n, TILE), lambda t, at: (0, 0)) for n in some],
                here,
                here,
                pl.BlockSpec((1, TILE, TILE), lambda t, at: (tiles, 0, 0)),
                pl.BlockSpec((TILE, TILE), lambda t, at: (0, 0)),
                pl.BlockSpec((TILE, panel), lambda t, at: (at[1] * tiles + tiles - 1, 0)),
            ],
            out_specs=[dealt, dealt],
            scratch_shapes=[pltpu.VMEM((count, panel), F32)] * 2,
        ),
        out_shape=[jax.ShapeDtypeStruct((2, slabs // 2, count, cols), kind) for kind in (F32, BF16)],
        compiler_params=params(),
        name="pair_products",
    )(at, band, *turned, *turned, *turned, *turned_right, modes, kphi, band, reach, modes)


class Places:
    def __init__(self, mesh):
        self.slabs = mesh.shape["slab"]
        self.panels = mesh.shape["blk"]
        self.group = self.slabs // self.panels
        self.all = [(s, b) for s in range(self.slabs) for b in range(self.panels)]

    def send(self, value, pairs):
        flat = [(s * self.panels + b, t * self.panels + c) for (s, b), (t, c) in pairs]
        return lax.ppermute(value, AXES, flat)

    def across(self, value, bit):
        return self.send(value, [((s, b), (s ^ bit, b)) for s, b in self.all])


def pick(array, index, axis=0):
    return lax.dynamic_index_in_dim(array, index, axis, keepdims=False)


def tie(value, *others):
    return lax.optimization_barrier((value, others))[0]


def body(places, modes, stiffness, offsets):
    rows, panel = modes.shape
    group, panels, slabs = places.group, places.panels, places.slabs
    cols = panel // group
    widths, groups = plan_of(cols)
    half = rows // 2
    slab, b = lax.axis_index("slab"), lax.axis_index("blk")
    p, core = slab // group, slab % 2
    one = lambda *values: jnp.stack([jnp.asarray(v, jnp.int32) for v in values])
    core_at, x_at, z_at, panel_at = one(core), one(slab // 2 % 2), one(slab // 4 % 2), one(jnp.where(p == b, 0, 1))
    zl = group // 4

    rights, ready = [], []
    for k in range(1, panels):
        pairs = []
        for s, c in places.all:
            other = (c - k) % panels
            if c < other:
                pairs.append(((s, other), (s, c)))
            elif s + 1 < slabs:
                pairs.append(((s + 1, other), (s, c)))
        tile = take_tile(modes, one(jnp.where((b + k) % panels < b, half // TILE, 0)))
        rights.append(places.send(tile, pairs))
    for k in range(1, panels):
        ready.append(turn(modes, half, one(jnp.where((b + k) % panels < b, 0, 1)), cols, widths))
    to_right = [((s, c), (s + 1, c)) for s, c in places.all if s + 1 < slabs]
    to_left = [(there, here) for here, there in to_right]
    left = places.send(tie(modes[rows - TILE :], ready), to_right)
    right = places.send(tie(modes[:TILE], ready), to_left)
    stiffness, ready = lax.optimization_barrier((stiffness, ready))
    band, first_band = expand(stiffness, offsets)
    reach = places.send(first_band, to_left)

    own = jnp.zeros((group, cols, cols), F32)
    cross = jnp.zeros((group, cols, cols), F32)
    for k in range(1, panels):
        other = (b - k) % panels
        source = (b + k) % panels
        at = one(core, jnp.where(b < other, 0, 1))
        there = [((s, c), (s, (c + k) % panels)) for s, c in places.all]
        same_core = [list(range(first, slabs, 2)) for first in range(2)]
        pieces = ready[k - 1]

        arrived = [places.send(pieces[0], there)]
        arrived.append(places.send(tie(pieces[1], arrived[0], left, right, rights, band), there))
        if k == 1:
            kphi = own_kphi(tie(band, rights, arrived[0]), modes, left, right)
        turned_rights = turn(rights[k - 1], TILE, one(0), cols, widths)
        arrived.append(places.send(tie(pieces[2], kphi), there))
        if k == 1:
            square = own_square(core_at, modes, tie(kphi, reach), cols)
        for piece in pieces[3:]:
            arrived.append(places.send(tie(piece, arrived[len(arrived) - 2]), there))

        def multiply(members, *gates):
            took = [tie(arrived[piece], *gates) for piece in members]
            tails = [turned_rights[piece] for piece in members]
            return pair_products(at, band, took, tails, modes, kphi, reach, cols, [widths[piece] for piece in members])

        def over_core(mine, theirs):
            return deal_out_sums(one(b, other), mine, places.across(theirs, 1), panels)

        def deal_out(parts):
            parts = parts.reshape(slabs // 2, *parts.shape[2:])
            return lax.all_to_all(parts, "slab", 0, 0, axis_index_groups=same_core)

        def gather_up(came, *gates):
            return gather_up_sums(tie(came, *gates)).reshape(group, -1, cols)

        def square_over(kept, given, bit, where, wire=BF16):
            shape = (-1, 2, *kept.shape[-2:])
            return fold(where, kept.reshape(shape), places.across(given, bit).reshape(shape), wire)

        def square_over_panels(kept, given):
            total = kept[0] + places.across(given, 4)[0].astype(F32) if group > 4 else kept[0]
            wire = total.astype(BF16)
            for d in range(1, panels):
                goal = lambda s: (s + d * group) % slabs
                pairs = [((s, c), (goal(s), c)) for s, c in places.all if goal(s) // group == c]
                total = total + places.send(wire, pairs).astype(F32)
            return total

        mine, theirs = multiply(groups[0], square[1])
        if k == 1:
            square_sum = square_over(*square, 1, x_at)
        first = over_core(mine, tie(theirs, arrived[groups[1][0]]))
        mine, theirs = multiply(groups[1], first, square_sum if k == 1 else ())
        first = gather_up(deal_out(first))
        second = over_core(mine, theirs)
        if k == 1:
            kept, given = square_sum
            square_sum = square_over(kept, given, 2, z_at) if group > 4 else [kept + places.across(given, 2).astype(F32)] * 2
        mine, theirs = multiply(groups[2], second)
        second = deal_out(second)
        third = deal_out(over_core(mine, tie(theirs, first, square_sum if k == 1 else ())))
        if k == 1:
            square_sum = square_over_panels(*square_sum)
        second = gather_up(second)
        third = gather_up(third, second)
        if k == 1:
            total_square = square_sum
        pairs = [((s, c), (s, (c - k) % panels)) for s, c in places.all if s // group == c]
        early = jnp.concatenate((first, second), 1)
        early_came = places.send(early, pairs)
        late = tie(third, early_came)
        came = jnp.concatenate([early_came, places.send(late, pairs)], 1)
        own = own + jnp.where(p == other, jnp.concatenate([early, late], 1), 0)
        cross = cross + jnp.where(p == source, came, 0)

    off = (jnp.swapaxes(own, 1, 2) + cross).reshape(panel, cols)
    return jnp.where(p == b, total_square, off)


def solution(mesh):
    in_specs = (P("slab", "blk"), P("slab", None), P("slab", None))
    out_specs = P("blk", "slab")
    return jax.shard_map(
        functools.partial(body, Places(mesh)), mesh=mesh, in_specs=in_specs, out_specs=out_specs, check_vma=False
    )
```
